32 devices in a mesh: region: 16 (over z, y, x), sta: 2 (over core).
Axes of the slice: x: 2, y: 2, z: 4, core: 2. Of those that a mesh axis runs over, the one named last changes fastest.
Arguments:
- waves: bfloat16 [8192, 32, 256], P('region', 'sta'), may hold values from -12 to 12
- partner: int32 [4], replicated, may hold values from 1 to 15, as said below
- send_rows: int32 [4, 1024], P(None, 'region'), may hold values from 0 to 511
- pair_local: int32 [4, 4096], P(None, 'region'), may hold values from 0 to 511
- pair_remote: int32 [4, 4096], P(None, 'region'), may hold values from 0 to 63
- station_mask: int32 [4, 4096, 32], P(None, 'region', 'sta'), may hold values from 0 to 1, as said below
- live_count: int32 [4, 16], P(None, 'region'), may hold values from 64 to 256, as said below
Outputs:
- correlation: float32 [4, 4096, 128], P(None, 'region', 'sta')
The draws below stay inside these ranges and needn't reach their ends.
Inputs may be any that keep to these rules, and one draw needn't show every extreme that they name: One round has partner 16 - 1. `station_mask`: every pair uses at least one station-channel. `live_count`: the live slots are the first ones; in every round some region has all 256 live.
All inputs are finite; a program needn't handle non-finite values.
Results may differ from the reference program's by a relative error of at most 0.003.
Values may be sent and summed in bfloat16 or wider, within the bound.
A program may use at most 128 MiB of HBM per device.

```python
import jax
import jax.numpy as jnp
from jax import lax

CH = 32
W = 256
NFFT = 512
LAGS = 128
ROUNDS = 4
EV_DEV = 512
REQ = 64
PAIRS = 256
N_REGION = 16


def draw_waves(key, part):
    key = jax.random.fold_in(key, 11)
    key_shape, key_amp, key_noise = jax.random.split(key, 3)
    shape = (N_REGION * EV_DEV, CH, W)
    template = jax.random.normal(key_shape, (CH, W), jnp.float32)
    amplitude = jax.random.uniform(key_amp, (N_REGION * EV_DEV, CH, 1), jnp.float32, -1.5, 1.5)
    noise = jax.random.normal(key_noise, shape, jnp.float32)
    return jnp.clip(amplitude * template[None, :, :] + noise, -12.0, 12.0).astype(jnp.bfloat16)


def draw_partner(key, part):
    key = jax.random.fold_in(key, 12)
    key_value, key_place = jax.random.split(key)
    values = jax.random.randint(key_value, (ROUNDS,), 1, N_REGION)
    place = jax.random.randint(key_place, (), 0, ROUNDS)
    return jnp.where(jnp.arange(ROUNDS) == place, N_REGION - 1, values).astype(jnp.int32)


def draw_station_mask(key, part):
    key = jax.random.fold_in(key, 13)
    shape = (ROUNDS, N_REGION * PAIRS, CH)
    levels = jax.random.randint(key, shape, 0, 4)
    turn_ids = jax.lax.broadcasted_iota(jnp.int32, shape, 0)
    pair_ids = jax.lax.broadcasted_iota(jnp.int32, shape, 1)
    chan_ids = jax.lax.broadcasted_iota(jnp.int32, shape, 2)
    forced = chan_ids == (pair_ids * 7 + turn_ids * 3) % CH
    return jnp.where((levels > 0) | forced, 1, 0).astype(jnp.int32)


def draw_live_count(key, part):
    key = jax.random.fold_in(key, 14)
    key_count, key_full = jax.random.split(key)
    counts = jax.random.randint(key_count, (ROUNDS, N_REGION), PAIRS // 4, PAIRS + 1)
    fullest = jax.random.randint(key_full, (ROUNDS, 1), 0, N_REGION)
    region_ids = jax.lax.broadcasted_iota(jnp.int32, (ROUNDS, N_REGION), 1)
    return jnp.where(region_ids == fullest, PAIRS, counts).astype(jnp.int32)


def touch_ends(array, stream_key, least, largest):
    dims = array.shape
    index_at = [jax.random.randint(jax.random.fold_in(stream_key, axis), (), 0, dims[axis]) for axis in range(len(dims))]
    array = array.at[tuple(index_at)].set(least)
    longest = dims.index(max(dims))
    index_at[longest] = (index_at[longest] + 1) % dims[longest]
    return array.at[tuple(index_at)].set(largest)


def setup_inputs(seed: int = 0) -> dict:
    seeds = jax.random.split(jax.random.key(seed), 8)
    waves = draw_waves(jax.random.fold_in(seeds[7], 71), 0)
    partner = draw_partner(jax.random.fold_in(seeds[7], 71), 0)
    send_rows = touch_ends(jax.random.randint(seeds[2], (ROUNDS, N_REGION * REQ), 0, EV_DEV), jax.random.fold_in(seeds[2], 1), 0, EV_DEV - 1).astype(jnp.int32)
    pair_local = touch_ends(jax.random.randint(seeds[3], (ROUNDS, N_REGION * PAIRS), 0, EV_DEV), jax.random.fold_in(seeds[3], 1), 0, EV_DEV - 1).astype(jnp.int32)
    pair_remote = touch_ends(jax.random.randint(seeds[4], (ROUNDS, N_REGION * PAIRS), 0, REQ), jax.random.fold_in(seeds[4], 1), 0, REQ - 1).astype(jnp.int32)
    station_mask = draw_station_mask(jax.random.fold_in(seeds[7], 71), 0)
    live_count = draw_live_count(jax.random.fold_in(seeds[7], 71), 0)
    return {"waves": waves, "partner": partner, "send_rows": send_rows, "pair_local": pair_local, "pair_remote": pair_remote, "station_mask": station_mask, "live_count": live_count}


epsilon = 1e-06
taper_edge = 32.0

def window_taper():
    sample_ids = jnp.arange(W, dtype=jnp.float32)
    edge_gap = jnp.minimum(sample_ids, W - 1 - sample_ids)
    return jnp.where(edge_gap < taper_edge, 0.5 - 0.5 * jnp.cos(jnp.pi * (edge_gap + 0.5) / taper_edge), 1.0)

def reference(waves, partner, send_rows, pair_local, pair_remote, station_mask, live_count):
    tapered = (waves.astype(jnp.float32) * window_taper()[None, None, :]).astype(jnp.bfloat16)
    energy = lax.optimization_barrier(jnp.sum(jnp.square(tapered.astype(jnp.float32)), axis=2))

    def one_region(region_id):
        results = []
        for turn in range(ROUNDS):
            partner_id = jnp.bitwise_xor(region_id, partner[turn]).astype(jnp.int32)
            row_ids = lax.dynamic_slice_in_dim(send_rows[turn], (partner_id * REQ).astype(jnp.int32), REQ) + partner_id * EV_DEV
            received = tapered[row_ids]
            received_energy = energy[row_ids]
            start = (region_id * PAIRS).astype(jnp.int32)
            local_ids = lax.dynamic_slice_in_dim(pair_local[turn], start, PAIRS) + region_id * EV_DEV
            remote_ids = lax.dynamic_slice_in_dim(pair_remote[turn], start, PAIRS)
            channel_mask = lax.dynamic_slice_in_dim(station_mask[turn], start, PAIRS).astype(jnp.float32)
            local_freq = jnp.fft.rfft(tapered[local_ids].astype(jnp.float32), n=NFFT, axis=-1)
            remote_freq = jnp.fft.rfft(received[remote_ids].astype(jnp.float32), n=NFFT, axis=-1)
            spectrum = lax.optimization_barrier(jnp.sum(channel_mask[:, :, None] * jnp.conj(local_freq) * remote_freq, axis=1))
            circular = jnp.fft.irfft(spectrum, n=NFFT, axis=-1)
            windowed = jnp.concatenate([circular[:, NFFT - LAGS // 2:], circular[:, :LAGS // 2]], axis=1)
            energy_a = lax.optimization_barrier(jnp.sum(channel_mask * energy[local_ids], axis=1))
            energy_b = lax.optimization_barrier(jnp.sum(channel_mask * received_energy[remote_ids], axis=1))
            normalized = windowed / jnp.sqrt(energy_a * energy_b + epsilon)[:, None]
            active = jnp.arange(PAIRS) < live_count[turn, region_id]
            results.append(jnp.where(active[:, None], normalized, 0.0))
        return jnp.stack(results)
    gathered = lax.map(one_region, jnp.arange(N_REGION, dtype=jnp.int32))
    return jnp.transpose(gathered, (1, 0, 2, 3)).reshape(ROUNDS, N_REGION * PAIRS, LAGS)
```

```python
import jax
import jax.numpy as jnp
import numpy as np
from jax import lax
from jax.experimental import pallas as pl
from jax.experimental.pallas import tpu as pltpu
from jax.sharding import PartitionSpec as P

LAGS = 128
GROUP = 32
epsilon = 1e-06
taper_edge = 32.0


def window_taper(samples):
    ids = np.arange(samples, dtype=np.float32)
    gap = np.minimum(ids, samples - 1 - ids)
    ramp = 0.5 - 0.5 * np.cos(np.pi * (gap + 0.5) / taper_edge)
    return np.where(gap < taper_edge, ramp, 1.0).astype(np.float32)[None, :]


def split(table):
    high = table.astype(np.float32).astype(jnp.bfloat16)
    low = (table - high.astype(np.float64)).astype(np.float32).astype(jnp.bfloat16)
    return high, low


def transform_tables(samples):
    size = 2 * samples
    half = samples
    t = np.arange(samples)[:, None]
    f = np.arange(half)[None, :]
    phase = (t * f % size) * (2.0 * np.pi / size)
    alternate = np.where(t % 2 == 0, 1.0, -1.0)
    forward = np.concatenate([np.cos(phase), alternate, -np.sin(phase[:, 1:])], axis=1)
    shift = (np.arange(LAGS) - LAGS // 2)[None, :]
    row = np.arange(half)[:, None]
    angle = (row * shift % size) * (2.0 * np.pi / size)
    lower = np.where(row == 0, 1.0, 2.0) / size * np.cos(angle)
    nyquist = np.where(shift % 2 == 0, 1.0, -1.0) / size
    upper = 2.0 * np.cos(angle[1:]) / size
    odd = np.where(row == 0, 0.0, -2.0 * np.sin(angle) / size)
    inverse = np.concatenate([lower, nyquist, upper, odd], axis=0)
    forward_parts = np.concatenate(split(forward), axis=0)
    inverse_parts = np.concatenate(split(inverse), axis=1)
    return forward_parts, inverse_parts


def pair_kernel(
    local_ids, remote_ids, waves, received, mask, taper, forward, inverse,
    raw, energy, remote_spec, remote_square, windows, spec, sums, squares
):
    channels, samples = waves.shape[1], waves.shape[2]
    requests = received.shape[1]
    pairs = raw.shape[1]
    half = samples // 2
    rows = GROUP * channels
    turn = pl.program_id(0)
    gain = jnp.broadcast_to(taper[...], (channels, samples))

    def transform(block):
        return jnp.dot(
            block, forward[:samples], preferred_element_type=jnp.float32
        ) + jnp.dot(block, forward[samples:], preferred_element_type=jnp.float32)

    def remote_group(step, carry):
        for g in range(GROUP):
            item = step * GROUP + g
            shaped = (received[0, item].astype(jnp.float32) * gain).astype(jnp.bfloat16)
            windows[pl.ds(g * channels, channels), :] = shaped
            wide = shaped.astype(jnp.float32)
            square = wide * wide
            remote_square[item] = square[:, :half] + square[:, half:]
        start = pl.multiple_of(step * rows, rows)
        remote_spec[pl.ds(start, rows), :] = transform(windows[...])
        return carry

    lax.fori_loop(0, requests // GROUP, remote_group, 0)

    def pair_group(step, carry):
        base = step * GROUP
        for g in range(GROUP):
            weight = jnp.broadcast_to(mask[0, step, :, g : g + 1], (channels, samples))
            first = waves[local_ids[turn, base + g]].astype(jnp.float32)
            shaped = (first * gain * weight).astype(jnp.bfloat16)
            windows[pl.ds(g * channels, channels), :] = shaped
            wide = shaped.astype(jnp.float32)
            total = jnp.sum(wide * wide, axis=0, keepdims=True)
            squares[0, g : g + 1, :] = total[:, :half] + total[:, half:]
            other = remote_square[remote_ids[turn, base + g]]
            squares[1, g : g + 1, :] = jnp.sum(other * weight[:, :half], axis=0, keepdims=True)
        spec[...] = transform(windows[...])
        for g in range(GROUP):
            at = pl.multiple_of(remote_ids[turn, base + g] * channels, channels)
            a = spec[pl.ds(g * channels, channels), :]
            b = remote_spec[pl.ds(at, channels), :]
            sums[g : g + 1, : 2 * samples] = jnp.sum(a * b, axis=0, keepdims=True)
            twist = a[:, :samples] * b[:, samples:] - a[:, samples:] * b[:, :samples]
            sums[g : g + 1, 2 * samples :] = jnp.sum(twist, axis=0, keepdims=True)
        total = sums[...]
        high = total.astype(jnp.bfloat16)
        low = (total - high.astype(jnp.float32)).astype(jnp.bfloat16)
        main = jnp.dot(high, inverse[...], preferred_element_type=jnp.float32)
        rest = jnp.dot(low, inverse[:, :LAGS], preferred_element_type=jnp.float32)
        out = pl.ds(pl.multiple_of(base, GROUP), GROUP)
        raw[0, out, :] = main[:, :LAGS] + main[:, LAGS:] + rest
        first_energy = jnp.sum(squares[0], axis=1, keepdims=True)
        second_energy = jnp.sum(squares[1], axis=1, keepdims=True)
        lane = lax.broadcasted_iota(jnp.int32, (GROUP, LAGS), 1)
        energy[0, out, :] = jnp.where(lane == 0, first_energy, second_energy)
        return carry

    lax.fori_loop(0, pairs // GROUP, pair_group, 0)


def correlate(waves, received, mask, local_ids, remote_ids, tables):
    forward, inverse, taper = tables
    events, channels, samples = waves.shape
    rounds, requests = received.shape[:2]
    pairs = local_ids.shape[1]
    groups = pairs // GROUP
    rows = GROUP * channels
    whole = lambda shape: pl.BlockSpec(shape, lambda r, *_: (0,) * len(shape))
    turn = lambda shape: pl.BlockSpec((1,) + shape, lambda r, *_: (r,) + (0,) * len(shape))
    flops = 2 * rounds * (requests + pairs) * channels * samples * 4 * samples
    return pl.pallas_call(
        pair_kernel,
        out_shape=[jax.ShapeDtypeStruct((rounds, pairs, LAGS), jnp.float32)] * 2,
        grid_spec=pltpu.PrefetchScalarGridSpec(
            num_scalar_prefetch=2,
            grid=(rounds,),
            in_specs=[
                whole(waves.shape),
                turn(received.shape[1:]),
                turn((groups, channels, GROUP)),
                whole(taper.shape),
                whole(forward.shape),
                whole(inverse.shape),
            ],
            out_specs=[turn((pairs, LAGS))] * 2,
            scratch_shapes=[
                pltpu.VMEM((requests * channels, 2 * samples), jnp.float32),
                pltpu.VMEM((requests, channels, samples // 2), jnp.float32),
                pltpu.VMEM((rows, samples), jnp.bfloat16),
                pltpu.VMEM((rows, 2 * samples), jnp.float32),
                pltpu.VMEM((GROUP, 3 * samples), jnp.float32),
                pltpu.VMEM((2, GROUP, samples // 2), jnp.float32),
            ],
        ),
        compiler_params=pltpu.CompilerParams(vmem_limit_bytes=40 * 2**20),
        cost_estimate=pl.CostEstimate(flops=flops, bytes_accessed=8 * 2**20, transcendentals=0),
    )(local_ids, remote_ids, waves, received, mask, taper, forward, inverse)


def exchange(payload, which):
    count = lax.axis_size("region")

    def hop(value):
        pairs = [(i, i ^ value) for i in range(count)]
        return lambda block: lax.ppermute(block, "region", pairs)

    return lax.switch(which - 1, [hop(v) for v in range(1, count)], payload)


def pad_channels(block, axis):
    extra = -block.shape[axis] % 16
    if extra == 0:
        return block
    widths = [(0, 0)] * block.ndim
    widths[axis] = (0, extra)
    return jnp.pad(block, widths)


def sum_over_stations(raw, energy):
    count = lax.axis_size("sta")
    me = lax.axis_index("sta")
    part = LAGS // count
    cut = lambda i: lax.dynamic_slice_in_dim(raw, i * part, part, axis=2)
    total, power = cut(me), energy
    for step in range(1, count):
        perm = [(i, (i + step) % count) for i in range(count)]
        total += lax.ppermute(cut((me + step) % count), "sta", perm)
        power += lax.ppermute(energy, "sta", perm)
    return total, power


def local(waves, partner, send_rows, pair_local, pair_remote, station_mask, live_count):
    samples = waves.shape[2]
    rounds, pairs = pair_local.shape
    tables = (*map(jnp.asarray, transform_tables(samples)), jnp.asarray(window_taper(samples)))
    outgoing = waves[send_rows]
    received = [exchange(outgoing[turn], partner[turn]) for turn in range(rounds)]
    mask = pad_channels(station_mask.astype(jnp.float32), 2)
    mask = mask.reshape(rounds, pairs // GROUP, GROUP, -1).swapaxes(2, 3)
    raw, energy = correlate(
        pad_channels(waves, 1), pad_channels(jnp.stack(received), 2), mask, pair_local, pair_remote, tables
    )
    total, power = sum_over_stations(raw, energy[..., :2])
    scaling = 1.0 / jnp.sqrt(power[..., 0] * power[..., 1] + epsilon)
    active = jnp.arange(pairs, dtype=jnp.int32)[None, :] < live_count
    return jnp.where(active[..., None], total * scaling[..., None], 0.0)


def solution(mesh):
    in_specs = (
        P("region", "sta", None),
        P(),
        P(None, "region"),
        P(None, "region"),
        P(None, "region"),
        P(None, "region", "sta"),
        P(None, "region"),
    )
    out_specs = P(None, "region", "sta")
    return jax.shard_map(local, mesh=mesh, in_specs=in_specs, out_specs=out_specs, check_vma=False)
```

```python
import jax
import jax.numpy as jnp
import numpy as np
from jax import lax
from jax.experimental import pallas as pl
from jax.experimental.pallas import tpu as pltpu
from jax.sharding import PartitionSpec as P

LAGS = 128
GROUP = 32
epsilon = 1e-06
taper_edge = 32.0


def window_taper(samples):
    ids = np.arange(samples, dtype=np.float32)
    gap = np.minimum(ids, samples - 1 - ids)
    ramp = 0.5 - 0.5 * np.cos(np.pi * (gap + 0.5) / taper_edge)
    return np.where(gap < taper_edge, ramp, 1.0).astype(np.float32)[None, :]


def split(table):
    high = table.astype(np.float32).astype(jnp.bfloat16)
    low = (table - high.astype(np.float64)).astype(np.float32).astype(jnp.bfloat16)
    return high, low


def transform_tables(samples):
    size = 2 * samples
    half = samples
    t = np.arange(samples)[:, None]
    f = np.arange(half)[None, :]
    phase = (t * f % size) * (2.0 * np.pi / size)
    alternate = np.where(t % 2 == 0, 1.0, -1.0)
    forward = np.concatenate([np.cos(phase), alternate, -np.sin(phase[:, 1:])], axis=1)
    shift = (np.arange(LAGS) - LAGS // 2)[None, :]
    row = np.arange(half)[:, None]
    angle = (row * shift % size) * (2.0 * np.pi / size)
    lower = np.where(row == 0, 1.0, 2.0) / size * np.cos(angle)
    nyquist = np.where(shift % 2 == 0, 1.0, -1.0) / size
    upper = 2.0 * np.cos(angle[1:]) / size
    odd = np.where(row == 0, 0.0, -2.0 * np.sin(angle) / size)
    inverse = np.concatenate([lower, nyquist, upper, odd], axis=0)
    forward_parts = np.concatenate(split(forward), axis=0)
    inverse_parts = np.concatenate(split(inverse), axis=1)
    return forward_parts, inverse_parts


def pair_kernel(
    local_ids, remote_ids, waves, received, mask, taper, forward, inverse,
    raw, energy, remote_spec, remote_square, windows, spec, sums, squares
):
    channels, samples = waves.shape[1], waves.shape[2]
    requests = received.shape[1]
    pairs = raw.shape[1]
    half = samples // 2
    rows = GROUP * channels
    turn = pl.program_id(0)
    gain = jnp.broadcast_to(taper[...], (channels, samples))

    def transform(block):
        return jnp.dot(
            block, forward[:samples], preferred_element_type=jnp.float32
        ) + jnp.dot(block, forward[samples:], preferred_element_type=jnp.float32)

    def remote_group(step, carry):
        for g in range(GROUP):
            item = step * GROUP + g
            shaped = (received[0, item].astype(jnp.float32) * gain).astype(jnp.bfloat16)
            windows[pl.ds(g * channels, channels), :] = shaped
            wide = shaped.astype(jnp.float32)
            square = wide * wide
            remote_square[item] = square[:, :half] + square[:, half:]
        start = pl.multiple_of(step * rows, rows)
        remote_spec[pl.ds(start, rows), :] = transform(windows[...])
        return carry

    lax.fori_loop(0, requests // GROUP, remote_group, 0)

    def pair_group(step, carry):
        base = step * GROUP
        for g in range(GROUP):
            weight = jnp.broadcast_to(mask[0, step, :, g : g + 1], (channels, samples))
            first = waves[local_ids[turn, base + g]].astype(jnp.float32)
            shaped = (first * gain * weight).astype(jnp.bfloat16)
            windows[pl.ds(g * channels, channels), :] = shaped
            wide = shaped.astype(jnp.float32)
            total = jnp.sum(wide * wide, axis=0, keepdims=True)
            squares[0, g : g + 1, :] = total[:, :half] + total[:, half:]
            other = remote_square[remote_ids[turn, base + g]]
            squares[1, g : g + 1, :] = jnp.sum(other * weight[:, :half], axis=0, keepdims=True)
        spec[...] = transform(windows[...])
        for g in range(GROUP):
            at = pl.multiple_of(remote_ids[turn, base + g] * channels, channels)
            a = spec[pl.ds(g * channels, channels), :]
            b = remote_spec[pl.ds(at, channels), :]
            sums[g : g + 1, : 2 * samples] = jnp.sum(a * b, axis=0, keepdims=True)
            twist = a[:, :samples] * b[:, samples:] - a[:, samples:] * b[:, :samples]
            sums[g : g + 1, 2 * samples :] = jnp.sum(twist, axis=0, keepdims=True)
        total = sums[...]
        high = total.astype(jnp.bfloat16)
        low = (total - high.astype(jnp.float32)).astype(jnp.bfloat16)
        main = jnp.dot(high, inverse[...], preferred_element_type=jnp.float32)
        rest = jnp.dot(low, inverse[:, :LAGS], preferred_element_type=jnp.float32)
        out = pl.ds(pl.multiple_of(base, GROUP), GROUP)
        raw[0, out, :] = main[:, :LAGS] + main[:, LAGS:] + rest
        first_energy = jnp.sum(squares[0], axis=1, keepdims=True)
        second_energy = jnp.sum(squares[1], axis=1, keepdims=True)
        lane = lax.broadcasted_iota(jnp.int32, (GROUP, LAGS), 1)
        energy[0, out, :] = jnp.where(lane == 0, first_energy, second_energy)
        return carry

    lax.fori_loop(0, pairs // GROUP, pair_group, 0)


def correlate(waves, received, mask, local_ids, remote_ids, tables):
    forward, inverse, taper = tables
    events, channels, samples = waves.shape
    rounds, requests = received.shape[:2]
    pairs = local_ids.shape[1]
    groups = pairs // GROUP
    rows = GROUP * channels
    whole = lambda shape: pl.BlockSpec(shape, lambda r, *_: (0,) * len(shape))
    turn = lambda shape: pl.BlockSpec((1,) + shape, lambda r, *_: (r,) + (0,) * len(shape))
    flops = 2 * rounds * (requests + pairs) * channels * samples * 4 * samples
    return pl.pallas_call(
        pair_kernel,
        out_shape=[jax.ShapeDtypeStruct((rounds, pairs, LAGS), jnp.float32)] * 2,
        grid_spec=pltpu.PrefetchScalarGridSpec(
            num_scalar_prefetch=2,
            grid=(rounds,),
            in_specs=[
                whole(waves.shape),
                turn(received.shape[1:]),
                turn((groups, channels, GROUP)),
                whole(taper.shape),
                whole(forward.shape),
                whole(inverse.shape),
            ],
            out_specs=[turn((pairs, LAGS))] * 2,
            scratch_shapes=[
                pltpu.VMEM((requests * channels, 2 * samples), jnp.float32),
                pltpu.VMEM((requests, channels, samples // 2), jnp.float32),
                pltpu.VMEM((rows, samples), jnp.bfloat16),
                pltpu.VMEM((rows, 2 * samples), jnp.float32),
                pltpu.VMEM((GROUP, 3 * samples), jnp.float32),
                pltpu.VMEM((2, GROUP, samples // 2), jnp.float32),
            ],
        ),
        compiler_params=pltpu.CompilerParams(vmem_limit_bytes=40 * 2**20),
        cost_estimate=pl.CostEstimate(flops=flops, bytes_accessed=8 * 2**20, transcendentals=0),
    )(local_ids, remote_ids, waves, received, mask, taper, forward, inverse)


def exchange(payload, which, work, operands):
    count = lax.axis_size("region")

    def hop(value):
        pairs = [(i, i ^ value) for i in range(count)]

        def branch(block, operands):
            return lax.ppermute(block, "region", pairs), work(operands)

        return branch

    return lax.switch(which - 1, [hop(v) for v in range(1, count)], payload, operands)


def pad_channels(block, axis):
    extra = -block.shape[axis] % 16
    if extra == 0:
        return block
    widths = [(0, 0)] * block.ndim
    widths[axis] = (0, extra)
    return jnp.pad(block, widths)


def sum_over_stations(raw, energy):
    count = lax.axis_size("sta")
    me = lax.axis_index("sta")
    part = LAGS // count
    cut = lambda i: lax.dynamic_slice_in_dim(raw, i * part, part, axis=2)
    total, power = cut(me), energy
    for step in range(1, count):
        perm = [(i, (i + step) % count) for i in range(count)]
        total += lax.ppermute(cut((me + step) % count), "sta", perm)
        power += lax.ppermute(energy, "sta", perm)
    return total, power


def local(waves, partner, send_rows, pair_local, pair_remote, station_mask, live_count):
    samples = waves.shape[2]
    rounds, pairs = pair_local.shape
    tables = (*map(jnp.asarray, transform_tables(samples)), jnp.asarray(window_taper(samples)))
    outgoing = waves[send_rows]
    mask = pad_channels(station_mask.astype(jnp.float32), 2)
    mask = mask.reshape(rounds, pairs // GROUP, GROUP, -1).swapaxes(2, 3)
    padded = pad_channels(waves, 1)

    @jax.jit
    def work(operands):
        block, turn_mask, first, second = operands
        return correlate(padded, pad_channels(block[None], 2), turn_mask, first, second, tables)

    def operands_of(turn, block):
        cut = slice(turn, turn + 1)
        return block, mask[cut], pair_local[cut], pair_remote[cut]

    block, _ = exchange(outgoing[0], partner[0], lambda operands: (), ())
    results = []
    for turn in range(1, rounds):
        block, result = exchange(
            outgoing[turn], partner[turn], work, operands_of(turn - 1, block)
        )
        results.append(result)
    results.append(work(operands_of(rounds - 1, block)))
    raw = jnp.concatenate([r[0] for r in results], axis=0)
    energy = jnp.concatenate([r[1][..., :2] for r in results], axis=0)
    total, power = sum_over_stations(raw, energy)
    scaling = 1.0 / jnp.sqrt(power[..., 0] * power[..., 1] + epsilon)
    active = jnp.arange(pairs, dtype=jnp.int32)[None, :] < live_count
    return jnp.where(active[..., None], total * scaling[..., None], 0.0)


def solution(mesh):
    in_specs = (
        P("region", "sta", None),
        P(),
        P(None, "region"),
        P(None, "region"),
        P(None, "region"),
        P(None, "region", "sta"),
        P(None, "region"),
    )
    out_specs = P(None, "region", "sta")
    return jax.shard_map(local, mesh=mesh, in_specs=in_specs, out_specs=out_specs, check_vma=False)
```

```python
import jax
import jax.numpy as jnp
import numpy as np
from jax import lax
from jax.experimental import pallas as pl
from jax.experimental.pallas import tpu as pltpu
from jax.sharding import PartitionSpec as P

LAGS = 128
GROUP = 64
UNROLL = 64
epsilon = 1e-06
taper_edge = 32.0


def window_taper(samples):
    ids = np.arange(samples, dtype=np.float32)
    gap = np.minimum(ids, samples - 1 - ids)
    ramp = 0.5 - 0.5 * np.cos(np.pi * (gap + 0.5) / taper_edge)
    return np.where(gap < taper_edge, ramp, 1.0).astype(np.float32)[None, :]


def split(table):
    high = table.astype(np.float32).astype(jnp.bfloat16)
    low = (table - high.astype(np.float64)).astype(np.float32).astype(jnp.bfloat16)
    return high, low


def transform_tables(samples):
    size = 2 * samples
    half = samples
    t = np.arange(samples)[:, None]
    f = np.arange(half)[None, :]
    phase = (t * f % size) * (2.0 * np.pi / size)
    alternate = np.where(t % 2 == 0, 1.0, -1.0)
    forward = np.concatenate([np.cos(phase), alternate, -np.sin(phase[:, 1:])], axis=1)
    shift = (np.arange(LAGS) - LAGS // 2)[None, :]
    row = np.arange(half)[:, None]
    angle = (row * shift % size) * (2.0 * np.pi / size)
    lower = np.where(row == 0, 1.0, 2.0) / size * np.cos(angle)
    nyquist = np.where(shift % 2 == 0, 1.0, -1.0) / size
    upper = 2.0 * np.cos(angle[1:]) / size
    odd = np.where(row == 0, 0.0, -2.0 * np.sin(angle) / size)
    inverse = np.concatenate([lower, nyquist, upper, odd], axis=0)
    forward_parts = np.concatenate(split(forward), axis=0)
    inverse_parts = np.concatenate(split(inverse), axis=1)
    return forward_parts, inverse_parts


def pair_kernel(
    local_ids, remote_ids, source, received, mask, taper, forward, inverse,
    raw, energy, waves, remote_spec, remote_square, windows, spec, sums, squares, sem
):
    fetch = pltpu.make_async_copy(source, waves, sem)
    fetch.start()
    channels, samples = waves.shape[1], waves.shape[2]
    requests = received.shape[1]
    pairs = raw.shape[1]
    half = samples // 2
    rows = GROUP * channels
    gain = jnp.broadcast_to(taper[...], (channels, samples))

    def transform(block):
        return jnp.dot(
            block, forward[:samples], preferred_element_type=jnp.float32
        ) + jnp.dot(block, forward[samples:], preferred_element_type=jnp.float32)

    def shape_remote(part, step):
        for g in range(UNROLL):
            item = step * GROUP + part * UNROLL + g
            shaped = (received[0, item].astype(jnp.float32) * gain).astype(jnp.bfloat16)
            at = pl.multiple_of((part * UNROLL + g) * channels, channels)
            windows[pl.ds(at, channels), :] = shaped
            wide = shaped.astype(jnp.float32)
            square = wide * wide
            remote_square[item] = square[:, :half] + square[:, half:]
        return step

    def remote_group(step, carry):
        lax.fori_loop(0, GROUP // UNROLL, shape_remote, step)
        start = pl.multiple_of(step * rows, rows)
        remote_spec[pl.ds(start, rows), :] = transform(windows[...])
        return carry

    lax.fori_loop(0, requests // GROUP, remote_group, 0)
    fetch.wait()

    def shape_local(part, step):
        own, other_rows = [], []
        for g in range(UNROLL):
            pair = step * GROUP + part * UNROLL + g
            block = step * (GROUP // UNROLL) + part
            weight = jnp.broadcast_to(mask[0, block, :, g : g + 1], (channels, half))
            twice = jnp.concatenate([weight, weight], axis=1)
            first = waves[local_ids[0, pair]].astype(jnp.float32)
            shaped = (first * gain * twice).astype(jnp.bfloat16)
            at = pl.multiple_of((part * UNROLL + g) * channels, channels)
            windows[pl.ds(at, channels), :] = shaped
            wide = shaped.astype(jnp.float32)
            square = wide * wide
            square = square[:, :half] + square[:, half:]
            own.append(jnp.sum(square, axis=0, keepdims=True))
            other = remote_square[remote_ids[0, pair]]
            other_rows.append(jnp.sum(other * weight, axis=0, keepdims=True))
        out = pl.ds(pl.multiple_of(part * UNROLL, UNROLL), UNROLL)
        squares[0, out, :] = jnp.concatenate(own, axis=0)
        squares[1, out, :] = jnp.concatenate(other_rows, axis=0)
        return step

    def multiply(part, step):
        mains, twists = [], []
        for g in range(UNROLL):
            at = pl.multiple_of((part * UNROLL + g) * channels, channels)
            item = remote_ids[0, step * GROUP + part * UNROLL + g]
            a = spec[pl.ds(at, channels), :]
            b = remote_spec[pl.ds(pl.multiple_of(item * channels, channels), channels), :]
            mains.append(jnp.sum(a * b, axis=0, keepdims=True))
            twist = a[:, :samples] * b[:, samples:] - a[:, samples:] * b[:, :samples]
            twists.append(jnp.sum(twist, axis=0, keepdims=True))
        out = pl.ds(pl.multiple_of(part * UNROLL, UNROLL), UNROLL)
        sums[out, : 2 * samples] = jnp.concatenate(mains, axis=0)
        sums[out, 2 * samples :] = jnp.concatenate(twists, axis=0)
        return step

    def pair_group(step, carry):
        lax.fori_loop(0, GROUP // UNROLL, shape_local, step)
        spec[...] = transform(windows[...])
        lax.fori_loop(0, GROUP // UNROLL, multiply, step)
        total = sums[...]
        high = total.astype(jnp.bfloat16)
        low = (total - high.astype(jnp.float32)).astype(jnp.bfloat16)
        main = jnp.dot(high, inverse[...], preferred_element_type=jnp.float32)
        rest = jnp.dot(low, inverse[:, :LAGS], preferred_element_type=jnp.float32)
        out = pl.ds(pl.multiple_of(step * GROUP, GROUP), GROUP)
        raw[0, out, :] = main[:, :LAGS] + main[:, LAGS:] + rest
        first_energy = jnp.sum(squares[0], axis=1, keepdims=True)
        second_energy = jnp.sum(squares[1], axis=1, keepdims=True)
        lane = lax.broadcasted_iota(jnp.int32, (GROUP, LAGS), 1)
        energy[0, out, :] = jnp.where(lane == 0, first_energy, second_energy)
        return carry

    lax.fori_loop(0, pairs // GROUP, pair_group, 0)


def correlate(waves, received, mask, local_ids, remote_ids, tables):
    forward, inverse, taper = tables
    events, channels, samples = waves.shape
    rounds, requests = received.shape[:2]
    pairs = local_ids.shape[1]
    groups = pairs // UNROLL
    rows = GROUP * channels
    whole = lambda shape: pl.BlockSpec(shape, lambda r, *_: (0,) * len(shape))
    turn = lambda shape: pl.BlockSpec((1,) + shape, lambda r, *_: (r,) + (0,) * len(shape))
    flops = 2 * rounds * (requests + pairs) * channels * samples * 4 * samples
    return pl.pallas_call(
        pair_kernel,
        out_shape=[jax.ShapeDtypeStruct((rounds, pairs, LAGS), jnp.float32)] * 2,
        grid_spec=pltpu.PrefetchScalarGridSpec(
            num_scalar_prefetch=2,
            grid=(rounds,),
            in_specs=[
                pl.BlockSpec(memory_space=pl.ANY),
                turn(received.shape[1:]),
                turn((groups, channels, UNROLL)),
                whole(taper.shape),
                whole(forward.shape),
                whole(inverse.shape),
            ],
            out_specs=[turn((pairs, LAGS))] * 2,
            scratch_shapes=[
                pltpu.VMEM(waves.shape, waves.dtype),
                pltpu.VMEM((requests * channels, 2 * samples), jnp.float32),
                pltpu.VMEM((requests, channels, samples // 2), jnp.float32),
                pltpu.VMEM((rows, samples), jnp.bfloat16),
                pltpu.VMEM((rows, 2 * samples), jnp.float32),
                pltpu.VMEM((GROUP, 3 * samples), jnp.float32),
                pltpu.VMEM((2, GROUP, samples // 2), jnp.float32),
                pltpu.SemaphoreType.DMA,
            ],
        ),
        compiler_params=pltpu.CompilerParams(vmem_limit_bytes=40 * 2**20),
        cost_estimate=pl.CostEstimate(flops=flops, bytes_accessed=8 * 2**20, transcendentals=0),
    )(local_ids, remote_ids, waves, received, mask, taper, forward, inverse)


def exchange(payload, which, work, operands):
    count = lax.axis_size("region")

    def hop(value):
        pairs = [(i, i ^ value) for i in range(count)]

        def branch(block, operands):
            return lax.ppermute(block, "region", pairs), work(operands)

        return branch

    return lax.switch(which - 1, [hop(v) for v in range(1, count)], payload, operands)


def pad_channels(block, axis):
    extra = -block.shape[axis] % 16
    if extra == 0:
        return block
    widths = [(0, 0)] * block.ndim
    widths[axis] = (0, extra)
    return jnp.pad(block, widths)


def sum_over_stations(raw, energy):
    count = lax.axis_size("sta")
    me = lax.axis_index("sta")
    part = LAGS // count
    cut = lambda i: lax.dynamic_slice_in_dim(raw, i * part, part, axis=2)
    total, power = cut(me), energy
    for step in range(1, count):
        perm = [(i, (i + step) % count) for i in range(count)]
        total += lax.ppermute(cut((me + step) % count), "sta", perm)
        power += lax.ppermute(energy, "sta", perm)
    return total, power


def local(waves, partner, send_rows, pair_local, pair_remote, station_mask, live_count):
    samples = waves.shape[2]
    rounds, pairs = pair_local.shape
    tables = (*map(jnp.asarray, transform_tables(samples)), jnp.asarray(window_taper(samples)))
    outgoing = waves[send_rows]
    mask = pad_channels(station_mask.astype(jnp.float32), 2)
    mask = mask.reshape(rounds, pairs // UNROLL, UNROLL, -1).swapaxes(2, 3)
    padded = pad_channels(waves, 1)

    @jax.jit
    def work(operands):
        block, turn_mask, first, second = operands
        return correlate(padded, pad_channels(block[None], 2), turn_mask, first, second, tables)

    def operands_of(turn, block):
        cut = slice(turn, turn + 1)
        return block, mask[cut], pair_local[cut], pair_remote[cut]

    block, _ = exchange(outgoing[0], partner[0], lambda operands: (), ())
    results = []
    for turn in range(1, rounds):
        block, result = exchange(
            outgoing[turn], partner[turn], work, operands_of(turn - 1, block)
        )
        results.append(result)
    results.append(work(operands_of(rounds - 1, block)))
    raw = jnp.concatenate([r[0] for r in results], axis=0)
    energy = jnp.concatenate([r[1][..., :2] for r in results], axis=0)
    total, power = sum_over_stations(raw, energy)
    scaling = 1.0 / jnp.sqrt(power[..., 0] * power[..., 1] + epsilon)
    active = jnp.arange(pairs, dtype=jnp.int32)[None, :] < live_count
    return jnp.where(active[..., None], total * scaling[..., None], 0.0)


def solution(mesh):
    in_specs = (
        P("region", "sta", None),
        P(),
        P(None, "region"),
        P(None, "region"),
        P(None, "region"),
        P(None, "region", "sta"),
        P(None, "region"),
    )
    out_specs = P(None, "region", "sta")
    return jax.shard_map(local, mesh=mesh, in_specs=in_specs, out_specs=out_specs, check_vma=False)
```

```python
import jax
import jax.numpy as jnp
import numpy as np
from jax import lax
from jax.experimental import pallas as pl
from jax.experimental.pallas import tpu as pltpu
from jax.sharding import PartitionSpec as P

LAGS = 128
GROUP = 32
UNROLL = 32
epsilon = 1e-06
taper_edge = 32.0


def window_taper(samples):
    ids = np.arange(samples, dtype=np.float32)
    gap = np.minimum(ids, samples - 1 - ids)
    ramp = 0.5 - 0.5 * np.cos(np.pi * (gap + 0.5) / taper_edge)
    return np.where(gap < taper_edge, ramp, 1.0).astype(np.float32)[None, :]


def split(table):
    high = table.astype(np.float32).astype(jnp.bfloat16)
    low = (table - high.astype(np.float64)).astype(np.float32).astype(jnp.bfloat16)
    return high, low


def transform_tables(samples):
    size = 2 * samples
    half = samples
    t = np.arange(samples)[:, None]
    f = np.arange(half)[None, :]
    phase = (t * f % size) * (2.0 * np.pi / size)
    alternate = np.where(t % 2 == 0, 1.0, -1.0)
    forward = np.concatenate([np.cos(phase), alternate, -np.sin(phase[:, 1:])], axis=1)
    shift = (np.arange(LAGS) - LAGS // 2)[None, :]
    row = np.arange(half)[:, None]
    angle = (row * shift % size) * (2.0 * np.pi / size)
    lower = np.where(row == 0, 1.0, 2.0) / size * np.cos(angle)
    nyquist = np.where(shift % 2 == 0, 1.0, -1.0) / size
    upper = 2.0 * np.cos(angle[1:]) / size
    odd = np.where(row == 0, 0.0, -2.0 * np.sin(angle) / size)
    inverse = np.concatenate([lower, nyquist, upper, odd], axis=0)
    forward_parts = np.concatenate(split(forward), axis=0)
    inverse_parts = np.concatenate(split(inverse), axis=1)
    return forward_parts, inverse_parts


def pair_kernel(
    local_ids, remote_ids, source, received, mask, taper, forward, inverse,
    raw, energy, waves, remote_spec, remote_square, windows, spec, sums, squares, sem
):
    fetch = pltpu.make_async_copy(source, waves, sem)
    fetch.start()
    channels, samples = waves.shape[1], waves.shape[2]
    requests = received.shape[1]
    pairs = raw.shape[1]
    half = samples // 2
    rows = GROUP * channels
    gain = jnp.broadcast_to(taper[...], (channels, samples))

    def transform(block):
        return jnp.dot(
            block, forward[:samples], preferred_element_type=jnp.float32
        ) + jnp.dot(block, forward[samples:], preferred_element_type=jnp.float32)

    def shape_remote(part, step):
        for g in range(UNROLL):
            item = step * GROUP + part * UNROLL + g
            shaped = (received[0, item].astype(jnp.float32) * gain).astype(jnp.bfloat16)
            at = pl.multiple_of((part * UNROLL + g) * channels, channels)
            windows[pl.ds(at, channels), :] = shaped
            wide = shaped.astype(jnp.float32)
            square = wide * wide
            remote_square[item] = square[:, :half] + square[:, half:]
        return step

    def remote_group(step, carry):
        lax.fori_loop(0, GROUP // UNROLL, shape_remote, step)
        start = pl.multiple_of(step * rows, rows)
        remote_spec[pl.ds(start, rows), :] = transform(windows[...])
        return carry

    lax.fori_loop(0, requests // GROUP, remote_group, 0)
    fetch.wait()

    def shape_local(part, step):
        own, other_rows = [], []
        for g in range(UNROLL):
            pair = step * GROUP + part * UNROLL + g
            block = step * (GROUP // UNROLL) + part
            weight = jnp.broadcast_to(mask[0, block, :, g : g + 1], (channels, half))
            twice = jnp.concatenate([weight, weight], axis=1)
            first = waves[local_ids[0, pair]].astype(jnp.float32)
            shaped = (first * gain * twice).astype(jnp.bfloat16)
            at = pl.multiple_of((part * UNROLL + g) * channels, channels)
            windows[pl.ds(at, channels), :] = shaped
            wide = shaped.astype(jnp.float32)
            square = wide * wide
            square = square[:, :half] + square[:, half:]
            own.append(jnp.sum(square, axis=0, keepdims=True))
            other = remote_square[remote_ids[0, pair]]
            other_rows.append(jnp.sum(other * weight, axis=0, keepdims=True))
        out = pl.ds(pl.multiple_of(part * UNROLL, UNROLL), UNROLL)
        squares[0, out, :] = jnp.concatenate(own, axis=0)
        squares[1, out, :] = jnp.concatenate(other_rows, axis=0)
        return step

    def multiply(part, step):
        mains, twists = [], []
        for g in range(UNROLL):
            at = pl.multiple_of((part * UNROLL + g) * channels, channels)
            item = remote_ids[0, step * GROUP + part * UNROLL + g]
            a = spec[pl.ds(at, channels), :]
            b = remote_spec[pl.ds(pl.multiple_of(item * channels, channels), channels), :]
            mains.append(jnp.sum(a * b, axis=0, keepdims=True))
            twist = a[:, :samples] * b[:, samples:] - a[:, samples:] * b[:, :samples]
            twists.append(jnp.sum(twist, axis=0, keepdims=True))
        out = pl.ds(pl.multiple_of(part * UNROLL, UNROLL), UNROLL)
        sums[out, : 2 * samples] = jnp.concatenate(mains, axis=0)
        sums[out, 2 * samples :] = jnp.concatenate(twists, axis=0)
        return step

    def pair_group(step, carry):
        lax.fori_loop(0, GROUP // UNROLL, shape_local, step)
        spec[...] = transform(windows[...])
        lax.fori_loop(0, GROUP // UNROLL, multiply, step)
        total = sums[...]
        high = total.astype(jnp.bfloat16)
        low = (total - high.astype(jnp.float32)).astype(jnp.bfloat16)
        main = jnp.dot(high, inverse[...], preferred_element_type=jnp.float32)
        rest = jnp.dot(low, inverse[:, :LAGS], preferred_element_type=jnp.float32)
        out = pl.ds(pl.multiple_of(step * GROUP, GROUP), GROUP)
        raw[0, out, :] = main[:, :LAGS] + main[:, LAGS:] + rest
        first_energy = jnp.sum(squares[0], axis=1, keepdims=True)
        second_energy = jnp.sum(squares[1], axis=1, keepdims=True)
        lane = lax.broadcasted_iota(jnp.int32, (GROUP, LAGS), 1)
        energy[0, out, :] = jnp.where(lane == 0, first_energy, second_energy)
        return carry

    lax.fori_loop(0, pairs // GROUP, pair_group, 0)


def correlate(waves, received, mask, local_ids, remote_ids, tables):
    forward, inverse, taper = tables
    events, channels, samples = waves.shape
    rounds, requests = received.shape[:2]
    pairs = local_ids.shape[1]
    groups = pairs // UNROLL
    rows = GROUP * channels
    whole = lambda shape: pl.BlockSpec(shape, lambda r, *_: (0,) * len(shape))
    turn = lambda shape: pl.BlockSpec((1,) + shape, lambda r, *_: (r,) + (0,) * len(shape))
    flops = 2 * rounds * (requests + pairs) * channels * samples * 4 * samples
    return pl.pallas_call(
        pair_kernel,
        out_shape=[jax.ShapeDtypeStruct((rounds, pairs, LAGS), jnp.float32)] * 2,
        grid_spec=pltpu.PrefetchScalarGridSpec(
            num_scalar_prefetch=2,
            grid=(rounds,),
            in_specs=[
                pl.BlockSpec(memory_space=pl.ANY),
                turn(received.shape[1:]),
                turn((groups, channels, UNROLL)),
                whole(taper.shape),
                whole(forward.shape),
                whole(inverse.shape),
            ],
            out_specs=[turn((pairs, LAGS))] * 2,
            scratch_shapes=[
                pltpu.VMEM(waves.shape, waves.dtype),
                pltpu.VMEM((requests * channels, 2 * samples), jnp.float32),
                pltpu.VMEM((requests, channels, samples // 2), jnp.float32),
                pltpu.VMEM((rows, samples), jnp.bfloat16),
                pltpu.VMEM((rows, 2 * samples), jnp.float32),
                pltpu.VMEM((GROUP, 3 * samples), jnp.float32),
                pltpu.VMEM((2, GROUP, samples // 2), jnp.float32),
                pltpu.SemaphoreType.DMA,
            ],
        ),
        compiler_params=pltpu.CompilerParams(vmem_limit_bytes=40 * 2**20),
        cost_estimate=pl.CostEstimate(flops=flops, bytes_accessed=8 * 2**20, transcendentals=0),
    )(local_ids, remote_ids, waves, received, mask, taper, forward, inverse)


def exchange(payload, which, work, operands):
    count = lax.axis_size("region")

    def hop(value):
        pairs = [(i, i ^ value) for i in range(count)]

        def branch(block, operands):
            return lax.ppermute(block, "region", pairs), work(operands)

        return branch

    return lax.switch(which - 1, [hop(v) for v in range(1, count)], payload, operands)


def pad_channels(block, axis):
    extra = -block.shape[axis] % 16
    if extra == 0:
        return block
    widths = [(0, 0)] * block.ndim
    widths[axis] = (0, extra)
    return jnp.pad(block, widths)


def sum_over_stations(raw, energy):
    count = lax.axis_size("sta")
    me = lax.axis_index("sta")
    part = LAGS // count
    cut = lambda i: lax.dynamic_slice_in_dim(raw, i * part, part, axis=2)
    total, power = cut(me), energy
    for step in range(1, count):
        perm = [(i, (i + step) % count) for i in range(count)]
        total += lax.ppermute(cut((me + step) % count), "sta", perm)
        power += lax.ppermute(energy, "sta", perm)
    return total, power


def local(waves, partner, send_rows, pair_local, pair_remote, station_mask, live_count):
    samples = waves.shape[2]
    rounds, pairs = pair_local.shape
    tables = (*map(jnp.asarray, transform_tables(samples)), jnp.asarray(window_taper(samples)))
    outgoing = waves[send_rows]
    mask = pad_channels(station_mask.astype(jnp.float32), 2)
    mask = mask.reshape(rounds, pairs // UNROLL, UNROLL, -1).swapaxes(2, 3)
    padded = pad_channels(waves, 1)

    @jax.jit
    def work(operands):
        block, turn_mask, first, second = operands
        return correlate(padded, pad_channels(block[None], 2), turn_mask, first, second, tables)

    def step(block, parts):
        sent, which, *rest = parts
        return exchange(sent, which, work, (block, *(part[None] for part in rest)))

    block, _ = exchange(outgoing[0], partner[0], lambda operands: (), ())
    lists = (mask, pair_local, pair_remote)
    block, (raw, energy) = lax.scan(
        step, block, (outgoing[1:], partner[1:], *(part[:-1] for part in lists))
    )
    last = work((block, *(part[-1:] for part in lists)))
    raw = jnp.concatenate([raw[:, 0], last[0]], axis=0)
    energy = jnp.concatenate([energy[:, 0, :, :2], last[1][..., :2]], axis=0)
    total, power = sum_over_stations(raw, energy)
    scaling = 1.0 / jnp.sqrt(power[..., 0] * power[..., 1] + epsilon)
    active = jnp.arange(pairs, dtype=jnp.int32)[None, :] < live_count
    return jnp.where(active[..., None], total * scaling[..., None], 0.0)


def solution(mesh):
    in_specs = (
        P("region", "sta", None),
        P(),
        P(None, "region"),
        P(None, "region"),
        P(None, "region"),
        P(None, "region", "sta"),
        P(None, "region"),
    )
    out_specs = P(None, "region", "sta")
    return jax.shard_map(local, mesh=mesh, in_specs=in_specs, out_specs=out_specs, check_vma=False)
```
